256 devices in a mesh: rep: 8 (over y, core), exp: 32 (over x, z).
Axes of the slice: x: 4, y: 4, z: 8, core: 2. Of those that a mesh axis runs over, the one named last changes fastest.
Arguments:
- grad_out: bfloat16 [8, 4096, 2048], P('rep', 'exp'), may hold values from -2 to 2
- gates: float32 [8, 4096, 8], P('rep', 'exp'), may hold values from 0.05 to 0.5
- routes: int32 [8, 4096, 8], P('rep', 'exp'), may hold values from 0 to 31, all different within a row; in each aligned block of 128 rows (0 to 127, 128 to 255, ..., all dimensions but the last counted through in order) at most 64 rows name the same one
- hidden: bfloat16 [8, 32, 2048, 768], P('rep', 'exp'), may hold values from -6 to 6
- error: bfloat16 [8, 32, 768, 2048], P('rep', 'exp'), may hold values from -6 to 6
- q_init: float32 [32, 32, 2048], P('exp'), may hold values from -6 to 6
Outputs:
- new_error: bfloat16 [8, 32, 768, 2048], P('rep', 'exp')
- p_factor: float32 [32, 32, 768], P('exp')
- q_factor: float32 [32, 32, 2048], P('exp')
The draws below stay inside these ranges and needn't reach their ends.
Inputs may be any that keep to these rules, and one draw needn't show every extreme that they name: `routes`: each row names 8 different experts; among the tokens of one device at most 64 name one expert, and in every draw exactly 64 do for some expert.
All inputs are finite; a program needn't handle non-finite values.
Results may differ from the reference program's by a relative error of at most 0.015.
Values may be sent and summed in bfloat16 or wider, within the bound.
No kernel may reach another device: no remote copies, remote signals or barrier semaphores. Data moves between devices by JAX's collectives and lax.ppermute only.
A program may use at most 128 MiB of HBM per device.

```python
import math
import jax
import jax.numpy as jnp
import numpy as np
from jax import lax

D = 2048
F = 768
RANK = 32
TOP = 8
TOK_DEV = 128
EXPERTS = 32
CAP = 64
SLOTS = 2048
TOKENS = 4096
REPLICAS = 8
N_EXP = 32


def block_scale(own_key, dims, cuts, least, high):
    loudness = 1.0
    for dim, parts in cuts:
        draws = jax.random.uniform(jax.random.fold_in(jax.random.fold_in(own_key, 6), dim), (parts,), jnp.float32, least / len(cuts), high / len(cuts))
        loudness = loudness * jnp.repeat(jnp.exp(draws), dims[dim] // parts).reshape((-1,) + (1,) * (len(dims) - 1 - dim))
    return loudness


def assign_block(key, own, number, rows, count, top, limit, slope):
    sequence = jax.random.permutation(key, count)
    crowded, usual = portions_of(count, rows * top, limit, slope, True), portions_of(count, rows * top, limit, slope, False)
    places = jnp.arange(count)

    def named(sizes, turn):
        used = int((sizes > 0).sum())
        fixed = max(1, used // 4)
        passed = fixed + (places - fixed + turn * (used - fixed)) % max(1, count - fixed)
        return jnp.zeros((count,), jnp.int32).at[sequence[jnp.where(places < fixed, places, passed)]].set(jnp.asarray(sizes, jnp.int32))

    sizes = jnp.where(number % 4 == 0, named(crowded, number // 4), named(usual, number - number // 4 - 1))
    mixed = jax.random.permutation(jax.random.fold_in(own, 3), count)
    source_of, receiver = mixed[0:count // 2 * 2:2], mixed[1:count // 2 * 2:2]
    margin = jnp.minimum(sizes[source_of] - 1, limit - sizes[receiver]) // 2
    margin = jnp.where((source_of == sequence[0]) | (receiver == sequence[0]) | (sizes[receiver] == 0), 0, jnp.maximum(margin, 0))
    passed = jax.random.randint(jax.random.fold_in(own, 4), (count // 2,), 0, 1 << 20) % (margin + 1)
    sizes = sizes.at[source_of].add(-passed).at[receiver].add(passed)
    members = jnp.searchsorted(jnp.cumsum(sizes), jnp.arange(rows * top), side="right").astype(jnp.int32)
    listing = members.reshape(top, rows).T
    listing = listing[jax.random.permutation(jax.random.fold_in(own, 1), rows)]
    turn = jax.random.randint(jax.random.fold_in(own, 2), (rows, 1), 0, top)
    return jnp.take_along_axis(listing, (jnp.arange(top)[None, :] + turn) % top, axis=1)


def portions_of(count, total, limit, lean, full):
    loads = [(1 << 20) // math.isqrt(rank ** lean) + 1 for rank in range(1, count + 1)]
    largest = limit if full else min(limit, max(-(-total // count), total * loads[0] // sum(loads)))
    least = 1 if total - largest >= count - 1 else 0
    given, rest = [largest] + [least] * (count - 1), total - largest - least * (count - 1)
    while rest > 0:
        free = [i for i in range(1, count) if given[i] < largest] or [i for i in range(1, count) if given[i] < limit]
        whole, left = sum([loads[i] for i in free]), rest
        for i in free:
            more = min(limit - given[i], max(1, left * loads[i] // whole), rest)
            given[i] = given[i] + more
            rest = rest - more
    return np.array(given)


def normal_values(key, extent, scale, most, pieces=(), held_as=jnp.bfloat16):
    factor_of = block_scale(key, extent, pieces, -0.22, 0.18) if pieces else 1.0
    array = jax.random.normal(key, extent, jnp.float32) * scale * factor_of
    return jnp.minimum(jnp.maximum(array, -most), most).astype(held_as)


def setup_inputs(seed: int = 0) -> dict:
    key_list = jax.random.split(jax.random.key(seed), 7)
    grad_out = normal_values(key_list[0], (REPLICAS, TOKENS, D), 0.25, 2.0, ((0, 8), (1, 32)))
    gates = jnp.clip(0.05 + 0.45 * jax.random.uniform(key_list[1], (REPLICAS, TOKENS, TOP), jnp.float32) ** block_scale(key_list[1], (REPLICAS, TOKENS, TOP), ((0, 8), (1, 32)), -0.2, 0.2), 0.05, 0.5)
    routes_keys = jax.random.split(jax.random.fold_in(key_list[2], 1), REPLICAS * TOKENS // TOK_DEV)
    routes_turns = jax.random.permutation(jax.random.fold_in(key_list[2], 3), REPLICAS * TOKENS // TOK_DEV)
    routes = jax.vmap(lambda own, number: assign_block(jax.random.fold_in(key_list[2], 2), own, number, TOK_DEV, EXPERTS, TOP, CAP, 2))(routes_keys, routes_turns).reshape((REPLICAS, TOKENS, TOP))
    hidden = normal_values(key_list[3], (REPLICAS, EXPERTS, SLOTS, F), 1.0, 6.0, ((0, 8), (1, 32)))
    error = normal_values(key_list[4], (REPLICAS, EXPERTS, F, D), 1.0, 6.0, ((0, 8), (1, 32)))
    q_init = normal_values(key_list[5], (EXPERTS, RANK, D), 1.0, 6.0, ((0, 32),), jnp.float32)
    return {"grad_out": grad_out, "gates": gates, "routes": routes, "hidden": hidden, "error": error, "q_init": q_init}


def inverse_slots(ids, weights, expert, cap, top):
    sources, count = ids.shape
    match = (ids == expert).astype(jnp.int32)
    position = jnp.cumsum(match, axis=1) - match
    source = jnp.arange(sources, dtype=jnp.int32)[:, None]
    total = sources * cap
    target = jnp.where(match > 0, source * cap + position, total).reshape(-1)
    token = (source * (count // top) + jnp.arange(count, dtype=jnp.int32)[None, :] // top).reshape(-1)
    token_slot = jnp.zeros((total,), jnp.int32).at[target].set(token.astype(jnp.int32), mode='drop')
    gate_slot = jnp.zeros((total,), jnp.float32).at[target].set(weights.reshape(-1), mode='drop')
    live_slot = jnp.zeros((total,), jnp.bool_).at[target].set(jnp.ones(target.shape, jnp.bool_), mode='drop')
    return (token_slot, gate_slot, live_slot)

def orthonormal(rows):
    count = rows.shape[0]
    index = jnp.arange(count, dtype=jnp.int32)

    def step(i, current):
        vector = current[i]
        vector = vector / jnp.sqrt(jnp.sum(vector * vector))
        coeffs = jnp.dot(current, vector, precision=lax.Precision.HIGHEST)
        current = current - jnp.where(index > i, coeffs, 0.0)[:, None] * vector[None, :]
        return current.at[i].set(vector)
    return lax.fori_loop(0, count, step, rows)

def reference(grad_out, gates, routes, hidden, error, q_init):
    ids = routes.reshape(REPLICAS, N_EXP, TOK_DEV * TOP)
    weights = gates.reshape(REPLICAS, N_EXP, TOK_DEV * TOP)

    def per_expert(expert):
        token_slot, gate_slot, live_slot = jax.vmap(lambda a, b: inverse_slots(a, b, expert, CAP, TOP))(ids, weights)
        rows = jax.vmap(lambda g, t: g[t])(grad_out, token_slot)
        scaled = (gate_slot[:, :, None] * rows.astype(jnp.float32)).astype(jnp.bfloat16)
        scaled = jnp.where(live_slot[:, :, None], scaled, jnp.zeros_like(scaled))
        held = lax.dynamic_index_in_dim(hidden, expert, 1, keepdims=False)
        grad_w = jnp.einsum('rsf,rsd->rfd', held.astype(jnp.float32), scaled.astype(jnp.float32))
        acc = grad_w + lax.dynamic_index_in_dim(error, expert, 1, keepdims=False).astype(jnp.float32)
        start = lax.dynamic_index_in_dim(q_init, expert, 0, keepdims=False)
        p_local = jnp.einsum('kd,rfd->rkf', start, acc, precision=lax.Precision.HIGHEST)
        p_hat = orthonormal(lax.optimization_barrier(jnp.sum(p_local, axis=0)))
        q_local = jnp.einsum('kf,rfd->rkd', p_hat, acc, precision=lax.Precision.HIGHEST)
        q_mean = lax.optimization_barrier(jnp.sum(q_local, axis=0)) / REPLICAS
        approx = jnp.einsum('kf,kd->fd', p_hat, q_mean, precision=lax.Precision.HIGHEST)
        return ((acc - approx[None]).astype(jnp.bfloat16), p_hat, q_mean)
    new_error, p_factor, q_factor = lax.map(per_expert, jnp.arange(EXPERTS, dtype=jnp.int32))
    return (jnp.transpose(new_error, (1, 0, 2, 3)), p_factor, q_factor)
```

```python
import functools

import jax
import jax.numpy as jnp
from jax import lax
from jax.experimental import pallas as pl
from jax.experimental.pallas import tpu as pltpu
from jax.sharding import PartitionSpec as P

F32 = jnp.float32
BF16 = jnp.bfloat16

NX, NZ = 4, 8
CB = 1280
DZ_ORDER = (0, 1, 7, 2, 6, 3, 5, 4)
GROUPS = ((0, 1, 7), (2, 6), (3, 5), (4,))


def shift(dx, dz):
    pairs = []
    for x in range(NX):
        for z in range(NZ):
            pairs.append((x * NZ + z, ((x + dx) % NX) * NZ + (z + dz) % NZ))
    return pairs


def move(block, dx, dz):
    return lax.ppermute(block, "exp", shift(dx, dz))


def place_kernel(order, expert, meta_ref, hidden_ref, out_ref):
    cap = hidden_ref.shape[0]
    routes = meta_ref[0, 0:8, :]
    gates = meta_ref[0, 8:16, :]
    tokens = routes.shape[1]
    match = routes == expert[0].astype(F32)
    gate = jnp.sum(jnp.where(match, gates, 0.0), axis=0, keepdims=True)
    live = jnp.sum(jnp.where(match, 1.0, 0.0), axis=0, keepdims=True)
    row = lax.broadcasted_iota(jnp.int32, (tokens, tokens), 0)
    col = lax.broadcasted_iota(jnp.int32, (tokens, tokens), 1)
    before = jnp.where(row < col, 1.0, 0.0).astype(BF16)
    live8 = jnp.broadcast_to(live, (8, tokens)).astype(BF16)
    position = jnp.dot(live8, before, preferred_element_type=F32)[0:1]
    slot = lax.broadcasted_iota(jnp.int32, (cap, tokens), 0).astype(F32)
    select = jnp.where((slot == position) & (live > 0.0), 1.0, 0.0).astype(BF16)
    placed = lax.dot_general(
        hidden_ref[...], select, (((0,), (0,)), ((), ())), preferred_element_type=F32
    )
    out_ref[...] = (placed * gate).astype(BF16)


def place(order, expert, meta, hidden):
    sources, _, tokens = meta.shape
    slots, width = hidden.shape
    cap = slots // sources
    return pl.pallas_call(
        place_kernel,
        grid_spec=pltpu.PrefetchScalarGridSpec(
            num_scalar_prefetch=2,
            grid=(sources,),
            in_specs=[
                pl.BlockSpec((1, 16, tokens), lambda i, order, expert: (order[i], 0, 0)),
                pl.BlockSpec((cap, width), lambda i, order, expert: (order[i], 0)),
            ],
            out_specs=pl.BlockSpec((width, tokens), lambda i, order, expert: (0, i)),
        ),
        out_shape=jax.ShapeDtypeStruct((width, sources * tokens), BF16),
        cost_estimate=pl.CostEstimate(
            flops=2 * slots * width * tokens * 4, bytes_accessed=10 << 20, transcendentals=0
        ),
        name="place",
    )(order, expert, meta, hidden)


def add_kernel(count, placed_ref, *refs):
    blocks, acc_ref, out_ref = refs[:count], refs[count], refs[count + 1]
    data = jnp.concatenate([b[...] for b in blocks], axis=0)
    out_ref[...] = acc_ref[...].astype(F32) + jnp.dot(
        placed_ref[...], data, preferred_element_type=F32
    )


def add_product(placed, start, blocks, acc, first_col, tile=256):
    count = len(blocks)
    tokens, cols = blocks[0].shape
    rows = placed.shape[0]
    part = lax.slice(placed, (0, start * tokens), (rows, (start + count) * tokens))
    base = first_col // tile
    in_place = acc.dtype == F32
    return pl.pallas_call(
        functools.partial(add_kernel, count),
        grid=(cols // tile,),
        in_specs=[pl.BlockSpec((rows, count * tokens), lambda i: (0, 0))]
        + [pl.BlockSpec((tokens, tile), lambda i: (0, i))] * count
        + [pl.BlockSpec((rows, tile), lambda i: (0, i + base))],
        out_specs=pl.BlockSpec((rows, tile), lambda i: (0, i + base)),
        out_shape=jax.ShapeDtypeStruct(acc.shape, F32),
        input_output_aliases={count + 1: 0} if in_place else {},
        cost_estimate=pl.CostEstimate(
            flops=2 * rows * count * tokens * cols,
            bytes_accessed=rows * cols * 8 + count * tokens * (cols + rows) * 2,
            transcendentals=0,
        ),
        compiler_params=pltpu.CompilerParams(vmem_limit_bytes=40 << 20),
        name="product",
    )(part, *blocks, acc)


def start_kernel(error_ref, out_ref):
    out_ref[...] = error_ref[...].astype(F32)


def ortho_kernel(a_ref, b_ref, c_ref, d_ref, out_ref):
    current = (a_ref[...] + b_ref[...]) + (c_ref[...] + d_ref[...])
    count = current.shape[0]
    row = lax.broadcasted_iota(jnp.int32, (count, 1), 0)
    for i in range(count):
        vector = current[i : i + 1, :]
        dots = jnp.sum(current * vector, axis=1, keepdims=True)
        norm2 = dots[i : i + 1, :]
        coeffs = jnp.where(row > i, dots / norm2, 0.0)
        scale = jnp.where(row == i, lax.rsqrt(norm2), 1.0)
        current = current * scale - coeffs * vector
    out_ref[...] = current


def orthonormal(parts):
    return pl.pallas_call(
        ortho_kernel,
        out_shape=jax.ShapeDtypeStruct(parts[0].shape, F32),
        name="orthonormal",
    )(*parts)


def partner(value, k):
    return lax.ppermute(value, "rep", [(i, i ^ k) for i in range(8)])


def gather_ring(grad):
    a = {(0, 0): grad[:, CB:]}
    b = {(0, 0): grad[:, :CB]}
    half = grad.shape[0] // 2
    a[1, 0] = move(a[0, 0], 1, 0)
    a[3, 0] = move(a[0, 0], -1, 0)
    b[0, 1] = move(b[0, 0], 0, 1)
    b[0, 7] = move(b[0, 0], 0, -1)
    a[2, 0] = move(a[0, 0], 2, 0)
    for k in (2, 3):
        b[0, k] = move(b[0, k - 1], 0, 1)
        b[0, 8 - k] = move(b[0, 9 - k], 0, -1)
    top = move(b[0, 3][:half], 0, 1)
    low = move(b[0, 5][half:], 0, -1)
    b[0, 4] = jnp.concatenate([top, low], axis=0)
    for n, dz in enumerate(DZ_ORDER):
        b[1, dz] = move(b[0, dz], 1, 0)
        b[3, dz] = move(b[0, dz], -1, 0)
        b[2, dz] = move(b[1, dz], 1, 0) if n % 2 == 0 else move(b[3, dz], -1, 0)
    for k in (1, 2, 3):
        for dx in range(NX):
            a[dx, k] = move(a[dx, k - 1], 0, 1)
            a[dx, 8 - k] = move(a[dx, (9 - k) % 8], 0, -1)
    for dx in range(NX):
        a[dx, 4] = move(a[dx, 3], 0, 1) if dx % 2 == 0 else move(a[dx, 5], 0, -1)
    return a, b


def body(grad_out, gates, routes, hidden, error, q_init):
    me = lax.axis_index("exp").astype(jnp.int32)
    x, z = me // NZ, me % NZ
    grad = grad_out[0]
    meta = jnp.concatenate([routes[0].astype(F32).T, gates[0].T], axis=0)
    meta = lax.all_gather(meta, "exp", axis=0, tiled=False)
    dx = jnp.tile(jnp.arange(NX, dtype=jnp.int32), NZ)
    dz = jnp.repeat(jnp.array(DZ_ORDER, jnp.int32), NX)
    order = ((x - dx) % NX) * NZ + (z - dz) % NZ
    placed = place(order, me.reshape(1), meta, hidden[0, 0])

    a, b = gather_ring(grad)
    acc = error[0, 0].astype(F32)
    start = 0
    for group in GROUPS:
        keys = [(i, k) for k in group for i in range(NX)]
        acc = add_product(placed, start, [b[key] for key in keys], acc, 0)
        acc = add_product(placed, start, [a[key] for key in keys], acc, CB)
        start += len(keys)

    q0 = q_init[0]
    p_local = jnp.einsum("kd,fd->kf", q0, acc, precision=lax.Precision.HIGHEST)
    p_chip = p_local + partner(p_local, 1)
    p_hat = orthonormal([p_chip, partner(p_chip, 2), partner(p_chip, 4), partner(p_chip, 6)])
    q_local = jnp.einsum("kf,fd->kd", p_hat, acc, precision=lax.Precision.HIGHEST)
    q_chip = (q_local + partner(q_local, 1)).astype(BF16)
    q2, q4, q6 = [partner(q_chip, k).astype(F32) for k in (2, 4, 6)]
    q_mean = ((q_chip.astype(F32) + q2) + (q4 + q6)) / 8.0
    approx = jnp.einsum("kf,kd->fd", p_hat, q_mean, precision=lax.Precision.HIGHEST)
    new_error = (acc - approx).astype(BF16)
    return new_error[None, None], p_hat[None], q_mean[None]


def solution(mesh):
    return jax.shard_map(
        body,
        mesh=mesh,
        in_specs=(
            P("rep", "exp", None),
            P("rep", "exp", None),
            P("rep", "exp", None),
            P("rep", "exp", None, None),
            P("rep", "exp", None, None),
            P("exp", None, None),
        ),
        out_specs=(P("rep", "exp", None, None), P("exp", None, None), P("exp", None, None)),
        check_vma=False,
    )
```

```python
import functools

import jax
import jax.numpy as jnp
from jax import lax
from jax.experimental import pallas as pl
from jax.experimental.pallas import tpu as pltpu
from jax.sharding import PartitionSpec as P

F32 = jnp.float32
BF16 = jnp.bfloat16

NX, NZ = 4, 8
TOK = 128
CAP = 64
META = 8
ROWS = TOK + META
GROUPS = ((0,), (1, 7), (2, 6), (3, 5), (4,))


def move(block, dx, dz):
    pairs = []
    for x in range(NX):
        for z in range(NZ):
            pairs.append((x * NZ + z, ((x + dx) % NX) * NZ + (z + dz) % NZ))
    return lax.ppermute(block, "exp", pairs)


def select_kernel(counts, experts, ids_ref, *refs):
    blocks, out_ref = refs[: len(counts)], refs[-1]
    total = sum(counts) * CAP
    row = lax.broadcasted_iota(jnp.int32, (TOK, TOK), 0)
    col = lax.broadcasted_iota(jnp.int32, (TOK, TOK), 1)
    before = jnp.where(row < col, 1.0, 0.0).astype(BF16)
    slot = lax.broadcasted_iota(jnp.int32, (CAP, TOK), 0).astype(F32)
    place = 0
    for ref, count in zip(blocks, counts):
        for b in range(count):
            base = b * ROWS
            meta = ref[base + TOK : base + ROWS, 0 : 4 * TOK].astype(F32)
            routes = meta[:, 0:TOK]
            gates = (meta[:, TOK : 2 * TOK] + meta[:, 2 * TOK : 3 * TOK]) + meta[:, 3 * TOK :]
            gate, live = [], []
            for e in range(experts):
                match = routes == ids_ref[e].astype(F32)
                gate.append(jnp.sum(jnp.where(match, gates, 0.0), axis=0, keepdims=True))
                live.append(jnp.sum(jnp.where(match, 1.0, 0.0), axis=0, keepdims=True))
            alive = jnp.concatenate(live + [jnp.zeros((8 - experts, TOK), F32)], axis=0)
            position = jnp.dot(alive.astype(BF16), before, preferred_element_type=F32)
            picks, scales = [], []
            for e in range(experts):
                pick = jnp.where((slot == position[e : e + 1]) & (live[e] > 0.0), 1.0, 0.0)
                picks.append(pick)
                scales.append(jnp.sum(pick * gate[e], axis=1, keepdims=True))
            pick = jnp.concatenate(picks, axis=0).astype(BF16)
            scale = jnp.concatenate(scales, axis=0)
            for c in range(0, ref.shape[1], 512):
                rows = jnp.dot(
                    pick, ref[base : base + TOK, c : c + 512], preferred_element_type=F32
                )
                rows = (rows * scale).astype(BF16)
                for e in range(experts):
                    first = e * total + place
                    out_ref[first : first + CAP, c : c + 512] = rows[e * CAP : (e + 1) * CAP]
            place += CAP


def select(blocks, ids, after=()):
    counts = tuple(b.shape[0] // ROWS for b in blocks)
    width = blocks[0].shape[1]
    experts = ids.shape[0]
    total = sum(counts)
    return pl.pallas_call(
        functools.partial(select_kernel, counts, experts),
        in_specs=[pl.BlockSpec(memory_space=pltpu.SMEM)]
        + [pl.BlockSpec(memory_space=pltpu.VMEM)] * len(blocks)
        + [pl.BlockSpec(memory_space=pl.ANY)] * len(after),
        out_specs=pl.BlockSpec(memory_space=pltpu.VMEM),
        out_shape=jax.ShapeDtypeStruct((experts * total * CAP, width), BF16),
        cost_estimate=pl.CostEstimate(
            flops=2 * total * experts * CAP * TOK * width,
            bytes_accessed=total * (ROWS + CAP * experts) * width * 2,
            transcendentals=0,
        ),
        compiler_params=pltpu.CompilerParams(vmem_limit_bytes=32 << 20),
        name="select",
    )(ids, *blocks, *after)


def pack_kernel(experts, ids_ref, grad_ref, routes_ref, gates_ref, block_ref, out_ref):
    gates = gates_ref[...]
    high = gates.astype(BF16)
    rest = gates - high.astype(F32)
    mid = rest.astype(BF16)
    low = (rest - mid.astype(F32)).astype(BF16)
    meta = jnp.concatenate([routes_ref[...].astype(F32).astype(BF16), high, mid, low], axis=1)
    block_ref[0:TOK, :] = grad_ref[...]
    block_ref[TOK:ROWS, 0 : 4 * TOK] = meta
    block_ref[TOK:ROWS, 4 * TOK :] = jnp.zeros((META, grad_ref.shape[1] - 4 * TOK), BF16)
    select_kernel((1,), experts, ids_ref, block_ref, out_ref)


def pack(grad, routes, gates, ids):
    vmem = pl.BlockSpec(memory_space=pltpu.VMEM)
    width = grad.shape[1]
    experts = ids.shape[0]
    return pl.pallas_call(
        functools.partial(pack_kernel, experts),
        in_specs=[pl.BlockSpec(memory_space=pltpu.SMEM)] + [vmem] * 3,
        out_specs=[vmem] * 2,
        out_shape=[
            jax.ShapeDtypeStruct((ROWS, width), BF16),
            jax.ShapeDtypeStruct((experts * CAP, width), BF16),
        ],
        cost_estimate=pl.CostEstimate(flops=0, bytes_accessed=2 << 20, transcendentals=0),
        compiler_params=pltpu.CompilerParams(vmem_limit_bytes=32 << 20),
        name="pack",
    )(ids, grad, routes, gates)


def split(value):
    high = value.astype(BF16)
    return high, (value - high.astype(F32)).astype(BF16)


def turn(order, hidden_ref, turned, sources):
    for j in range(sources // 2):
        pair = [
            hidden_ref[pl.ds(pl.multiple_of(order[2 * j + k] * CAP, CAP), CAP), :] for k in range(2)
        ]
        turned[:, j * 2 * CAP : (j + 1) * 2 * CAP] = jnp.concatenate(pair, axis=0).T


def left(acc, q_ref, total_ref):
    rank = q_ref.shape[1] // 2
    high, low = split(acc)
    both = jnp.dot(high, q_ref[...], preferred_element_type=F32)
    rest = jnp.dot(low, q_ref[:, :rank], preferred_element_type=F32)
    total_ref[...] += both[:, :rank] + (both[:, rank:] + rest)
    return high, low


def product_kernel(count, sources, order, hidden_ref, *refs):
    parts = refs[:count]
    init_ref, q_ref, acc_ref, p_ref, turned = refs[count:]

    @pl.when(pl.program_id(0) == 0)
    def _():
        p_ref[...] = jnp.zeros_like(p_ref)
        turn(order, hidden_ref, turned, sources)

    data = jnp.concatenate([p[...] for p in parts], axis=0)
    acc = init_ref[...].astype(F32) + jnp.dot(turned[...], data, preferred_element_type=F32)
    acc_ref[...] = acc
    left(acc, q_ref, p_ref)


def first_kernel(count, sources, order, hidden_ref, *refs):
    parts = refs[:count]
    init_ref, acc_ref, turned = refs[count:]

    @pl.when(pl.program_id(0) == 0)
    def _():
        turn(order, hidden_ref, turned, sources)

    data = jnp.concatenate([p[...] for p in parts], axis=0)
    acc_ref[...] = init_ref[...].astype(F32) + jnp.dot(
        turned[...], data, preferred_element_type=F32
    )


def product(order, hidden, parts, init, q_turned=None, first=0, tile=256):
    rows = init.shape[0]
    slots, feats = hidden.shape
    sources = order.shape[0]
    width = parts[0].shape[1]
    base = first // tile
    in_specs = [pl.BlockSpec((slots, feats), lambda i, order: (0, 0))]
    in_specs += [pl.BlockSpec((p.shape[0], tile), lambda i, order: (0, i)) for p in parts]
    in_specs += [pl.BlockSpec((rows, tile), lambda i, order: (0, i + base))]
    out_specs = [pl.BlockSpec((rows, tile), lambda i, order: (0, i))]
    out_shape = [jax.ShapeDtypeStruct((rows, width), F32)]
    args = (order, hidden, *parts, init)
    kernel = first_kernel
    if q_turned is not None:
        kernel = product_kernel
        thin = q_turned.shape[1]
        in_specs += [pl.BlockSpec((tile, thin), lambda i, order: (i + base, 0))]
        out_specs += [pl.BlockSpec((rows, thin // 2), lambda i, order: (0, 0))]
        out_shape += [jax.ShapeDtypeStruct((rows, thin // 2), F32)]
        args += (q_turned,)
    return pl.pallas_call(
        functools.partial(kernel, len(parts), sources),
        grid_spec=pltpu.PrefetchScalarGridSpec(
            num_scalar_prefetch=1,
            grid=(width // tile,),
            in_specs=in_specs,
            out_specs=out_specs,
            scratch_shapes=[pltpu.VMEM((feats, sources * CAP), BF16)],
        ),
        out_shape=out_shape,
        cost_estimate=pl.CostEstimate(
            flops=2 * feats * sources * CAP * width,
            bytes_accessed=rows * width * 8 + sources * CAP * (feats + width) * 2,
            transcendentals=0,
        ),
        compiler_params=pltpu.CompilerParams(vmem_limit_bytes=40 << 20),
        name="product",
    )(*args)


def left_kernel(count, sources, order, hidden_hbm, *refs):
    parts = refs[:count]
    q_ref, p_ref, out_ref, held, sem = refs[count:]
    copies = [
        pltpu.make_async_copy(
            hidden_hbm.at[pl.ds(pl.multiple_of(order[j] * CAP, CAP), CAP)],
            held.at[pl.ds(j * CAP, CAP)],
            sem.at[j],
        )
        for j in range(sources)
    ]
    for copy in copies:
        copy.start()
    data = jnp.concatenate([p[...] for p in parts], axis=0)
    rank = out_ref.shape[0]
    both = jnp.dot(data, q_ref[...], preferred_element_type=F32)
    high, low = split(both[:, :rank] + both[:, rank:])
    for copy in copies:
        copy.wait()
    more = lax.dot_general(
        jnp.concatenate([high, low], axis=1),
        held[...],
        (((0,), (0,)), ((), ())),
        preferred_element_type=F32,
    )
    out_ref[...] = p_ref[...].T + (more[:rank] + more[rank:])


def left_last(order, hidden, parts, q_turned, p_rest):
    vmem = pl.BlockSpec(memory_space=pltpu.VMEM)
    sources = order.shape[0]
    feats = hidden.shape[1]
    return pl.pallas_call(
        functools.partial(left_kernel, len(parts), sources),
        in_specs=[pl.BlockSpec(memory_space=pltpu.SMEM), pl.BlockSpec(memory_space=pl.ANY)]
        + [vmem] * (len(parts) + 2),
        out_specs=vmem,
        out_shape=jax.ShapeDtypeStruct(p_rest.shape[::-1], F32),
        scratch_shapes=[
            pltpu.VMEM((sources * CAP, feats), BF16),
            pltpu.SemaphoreType.DMA((sources,)),
        ],
        compiler_params=pltpu.CompilerParams(vmem_limit_bytes=16 << 20),
        name="left_last",
    )(order, hidden, *parts, q_turned, p_rest)


def tail_kernel(sources, order, hidden_ref, *refs):
    part_ref, acc_ref, high_ref, low_ref, turned = refs

    @pl.when(pl.program_id(0) == 0)
    def _():
        turn(order, hidden_ref, turned, sources)

    acc = acc_ref[...] + jnp.dot(turned[...], part_ref[...], preferred_element_type=F32)
    high_ref[...], low_ref[...] = split(acc)


def tail(order, hidden, part, acc, tile=256):
    rows, width = acc.shape
    slots, feats = hidden.shape
    sources = order.shape[0]
    flat = pl.BlockSpec((rows, tile), lambda i, order: (0, i))
    return pl.pallas_call(
        functools.partial(tail_kernel, sources),
        grid_spec=pltpu.PrefetchScalarGridSpec(
            num_scalar_prefetch=1,
            grid=(width // tile,),
            in_specs=[pl.BlockSpec((slots, feats), lambda i, order: (0, 0))]
            + [pl.BlockSpec((part.shape[0], tile), lambda i, order: (0, i)), flat],
            out_specs=[flat, flat],
            scratch_shapes=[pltpu.VMEM((feats, sources * CAP), BF16)],
        ),
        out_shape=[jax.ShapeDtypeStruct((rows, width), BF16)] * 2,
        cost_estimate=pl.CostEstimate(
            flops=2 * feats * sources * CAP * width,
            bytes_accessed=rows * width * 8 + sources * CAP * (feats + width) * 2,
            transcendentals=0,
        ),
        compiler_params=pltpu.CompilerParams(vmem_limit_bytes=32 << 20),
        name="tail",
    )(order, hidden, part, acc)


def factors_kernel(a_ref, b_ref, c_ref, d_ref, high_hbm, low_hbm, p_ref, q_ref, high, low, sems):
    copies = [
        pltpu.make_async_copy(high_hbm, high, sems.at[0]),
        pltpu.make_async_copy(low_hbm, low, sems.at[1]),
    ]
    for copy in copies:
        copy.start()
    current = (a_ref[...] + b_ref[...]) + (c_ref[...] + d_ref[...])
    count = current.shape[0]
    row = lax.broadcasted_iota(jnp.int32, (count, 1), 0)
    for i in range(count):
        vector = current[i : i + 1, :]
        dots = jnp.sum(current * vector, axis=1, keepdims=True)
        norm2 = dots[i : i + 1, :]
        coeffs = jnp.where(row > i, dots / norm2, 0.0)
        scale = jnp.where(row == i, lax.rsqrt(norm2), 1.0)
        current = current * scale - coeffs * vector
    p_ref[...] = current
    p_high = current.astype(BF16)
    p_low = (current - p_high.astype(F32)).astype(BF16)
    p_both = jnp.concatenate([p_high, p_low], axis=0)
    for copy in copies:
        copy.wait()
    for c in range(0, q_ref.shape[1], 512):
        both = jnp.dot(p_both, high[:, c : c + 512], preferred_element_type=F32)
        rest = jnp.dot(p_high, low[:, c : c + 512], preferred_element_type=F32)
        q_ref[:, c : c + 512] = both[:count] + (both[count:] + rest)


def factors(parts, high, low):
    rank = parts[0].shape[0]
    rows, width = high.shape
    vmem, far = pl.BlockSpec(memory_space=pltpu.VMEM), pl.BlockSpec(memory_space=pl.ANY)
    return pl.pallas_call(
        factors_kernel,
        in_specs=[vmem] * 4 + [far] * 2,
        out_specs=[vmem] * 2,
        out_shape=[
            jax.ShapeDtypeStruct((rank, rows), F32),
            jax.ShapeDtypeStruct((rank, width), F32),
        ],
        scratch_shapes=[
            pltpu.VMEM((rows, width), BF16),
            pltpu.VMEM((rows, width), BF16),
            pltpu.SemaphoreType.DMA((2,)),
        ],
        compiler_params=pltpu.CompilerParams(vmem_limit_bytes=24 << 20),
        name="factors",
    )(*parts, high, low)


def finish_kernel(p_ref, a_ref, b_ref, c_ref, d_ref, high_ref, low_ref, out_ref, q_ref):
    q = (a_ref[...].astype(F32) + b_ref[...].astype(F32)) + (
        c_ref[...].astype(F32) + d_ref[...].astype(F32)
    )
    q = q * 0.125
    q_ref[...] = q
    q_high = q.astype(BF16)
    q_low = (q - q_high.astype(F32)).astype(BF16)
    p = p_ref[...]
    p_high = p.astype(BF16)
    p_low = (p - p_high.astype(F32)).astype(BF16)
    approx = lax.dot_general(
        jnp.concatenate([p_high, p_high, p_low], axis=0),
        jnp.concatenate([q_high, q_low, q_high], axis=0),
        (((0,), (0,)), ((), ())),
        preferred_element_type=F32,
    )
    acc = high_ref[...].astype(F32) + low_ref[...].astype(F32)
    out_ref[...] = (acc - approx).astype(BF16)


def finish(p_hat, parts, high, low, tile=256):
    rank, rows = p_hat.shape
    width = high.shape[1]
    flat = pl.BlockSpec((rows, tile), lambda i: (0, i))
    thin = pl.BlockSpec((rank, tile), lambda i: (0, i))
    return pl.pallas_call(
        finish_kernel,
        grid=(width // tile,),
        in_specs=[pl.BlockSpec((rank, rows), lambda i: (0, 0))] + [thin] * 4 + [flat] * 2,
        out_specs=[flat, thin],
        out_shape=[
            jax.ShapeDtypeStruct((rows, width), BF16),
            jax.ShapeDtypeStruct((rank, width), F32),
        ],
        compiler_params=pltpu.CompilerParams(vmem_limit_bytes=16 << 20),
        name="finish",
    )(p_hat, *parts, high, low)


def partner(value, k):
    return lax.ppermute(value, "rep", [(i, i ^ k) for i in range(8)])


def body(grad_out, gates, routes, hidden, error, q_init):
    me = lax.axis_index("exp").astype(jnp.int32)
    x, z = me // NZ, me % NZ
    ids = jnp.arange(NX, dtype=jnp.int32) * NZ + z
    own, sent = pack(grad_out[0], routes[0].T, gates[0].T, ids)

    b = {0: own}
    parts, order = [], []
    columns = [[i * NZ + k for i in range(NX)] for k in range(NZ)]

    def spread(group, sent):
        parts.append(
            lax.all_to_all(
                sent, "exp", split_axis=0, concat_axis=0, tiled=True, axis_index_groups=columns
            )
        )
        dx = jnp.array([i for i in range(NX) for k in group], jnp.int32)
        dz = jnp.array([k for i in range(NX) for k in group], jnp.int32)
        order.append(dx * NZ + (z - dz) % NZ)

    b[1] = move(b[0], 0, 1)
    b[7] = move(b[0], 0, -1)
    b[2] = move(b[1], 0, 1)
    b[6] = move(b[7], 0, -1)
    b[3] = move(b[2], 0, 1)
    b[5] = move(b[6], 0, -1)
    b[4] = move(b[3], 0, 1)
    spread(GROUPS[0], sent)
    for group in GROUPS[1:4]:
        spread(group, select([b[k] for k in group], ids))
    held = hidden[0, 0]
    q_turned = jnp.concatenate(split(q_init[0]), axis=0).T
    (acc,) = product(jnp.concatenate(order[:3]), held, parts[:3], error[0, 0])
    spread(GROUPS[4], select([b[k] for k in GROUPS[4]], ids, (acc,)))
    acc, p_rest = product(order[3], held, parts[3:4], acc, q_turned)
    p_local = left_last(order[-1], held, parts[-1:], q_turned, p_rest)
    p_chip = p_local + partner(p_local, 1)
    p_parts = [p_chip] + [partner(p_chip, k) for k in (2, 4, 6)]
    high, low = tail(order[-1], held, parts[-1], acc)
    p_hat, q_local = factors(p_parts, high, low)
    q_chip = (q_local + partner(q_local, 1)).astype(BF16)
    new_error, q_mean = finish(p_hat, [q_chip] + [partner(q_chip, k) for k in (2, 4, 6)], high, low)
    return new_error[None, None], p_hat[None], q_mean[None]


def solution(mesh):
    return jax.shard_map(
        body,
        mesh=mesh,
        in_specs=(
            P("rep", "exp", None),
            P("rep", "exp", None),
            P("rep", "exp", None),
            P("rep", "exp", None, None),
            P("rep", "exp", None, None),
            P("exp", None, None),
        ),
        out_specs=(P("rep", "exp", None, None), P("exp", None, None), P("exp", None, None)),
        check_vma=False,
    )
```

```python
import functools

import jax
import jax.numpy as jnp
from jax import lax
from jax.experimental import pallas as pl
from jax.experimental.pallas import tpu as pltpu
from jax.sharding import PartitionSpec as P

F32 = jnp.float32
BF16 = jnp.bfloat16

NX, NZ = 4, 8
TOK = 128
CAP = 64
META = 8
ROWS = TOK + META
GROUPS = ((0,), (1, 7), (2, 6), (3, 5), (4,))


def move(block, dx, dz):
    pairs = []
    for x in range(NX):
        for z in range(NZ):
            pairs.append((x * NZ + z, ((x + dx) % NX) * NZ + (z + dz) % NZ))
    return lax.ppermute(block, "exp", pairs)


def select_kernel(counts, experts, ids_ref, *refs):
    blocks, out_ref = refs[: len(counts)], refs[-1]
    total = sum(counts) * CAP
    row = lax.broadcasted_iota(jnp.int32, (TOK, TOK), 0)
    col = lax.broadcasted_iota(jnp.int32, (TOK, TOK), 1)
    before = jnp.where(row < col, 1.0, 0.0).astype(BF16)
    slot = lax.broadcasted_iota(jnp.int32, (CAP, TOK), 0).astype(F32)
    place = 0
    for ref, count in zip(blocks, counts):
        for b in range(count):
            base = b * ROWS
            meta = ref[base + TOK : base + ROWS, 0 : 4 * TOK].astype(F32)
            routes = meta[:, 0:TOK]
            gates = (meta[:, TOK : 2 * TOK] + meta[:, 2 * TOK : 3 * TOK]) + meta[:, 3 * TOK :]
            gate, live = [], []
            for e in range(experts):
                match = routes == ids_ref[e].astype(F32)
                gate.append(jnp.sum(jnp.where(match, gates, 0.0), axis=0, keepdims=True))
                live.append(jnp.sum(jnp.where(match, 1.0, 0.0), axis=0, keepdims=True))
            alive = jnp.concatenate(live + [jnp.zeros((8 - experts, TOK), F32)], axis=0)
            position = jnp.dot(alive.astype(BF16), before, preferred_element_type=F32)
            picks, scales = [], []
            for e in range(experts):
                pick = jnp.where((slot == position[e : e + 1]) & (live[e] > 0.0), 1.0, 0.0)
                picks.append(pick)
                scales.append(jnp.sum(pick * gate[e], axis=1, keepdims=True))
            pick = jnp.concatenate(picks, axis=0).astype(BF16)
            scale = jnp.concatenate(scales, axis=0)
            for c in range(0, ref.shape[1], 512):
                rows = jnp.dot(
                    pick, ref[base : base + TOK, c : c + 512], preferred_element_type=F32
                )
                rows = (rows * scale).astype(BF16)
                for e in range(experts):
                    first = e * total + place
                    out_ref[first : first + CAP, c : c + 512] = rows[e * CAP : (e + 1) * CAP]
            place += CAP


def select(blocks, ids, after=()):
    counts = tuple(b.shape[0] // ROWS for b in blocks)
    width = blocks[0].shape[1]
    experts = ids.shape[0]
    total = sum(counts)
    return pl.pallas_call(
        functools.partial(select_kernel, counts, experts),
        in_specs=[pl.BlockSpec(memory_space=pltpu.SMEM)]
        + [pl.BlockSpec(memory_space=pltpu.VMEM)] * len(blocks)
        + [pl.BlockSpec(memory_space=pl.ANY)] * len(after),
        out_specs=pl.BlockSpec(memory_space=pltpu.VMEM),
        out_shape=jax.ShapeDtypeStruct((experts * total * CAP, width), BF16),
        cost_estimate=pl.CostEstimate(
            flops=2 * total * experts * CAP * TOK * width,
            bytes_accessed=total * (ROWS + CAP * experts) * width * 2,
            transcendentals=0,
        ),
        compiler_params=pltpu.CompilerParams(vmem_limit_bytes=32 << 20),
        name="select",
    )(ids, *blocks, *after)


def pack_kernel(grad_ref, routes_ref, gates_ref, block_ref):
    gates = gates_ref[...]
    high = gates.astype(BF16)
    rest = gates - high.astype(F32)
    mid = rest.astype(BF16)
    low = (rest - mid.astype(F32)).astype(BF16)
    meta = jnp.concatenate([routes_ref[...].astype(F32).astype(BF16), high, mid, low], axis=1)
    block_ref[0:TOK, :] = grad_ref[...]
    block_ref[TOK:ROWS, 0 : 4 * TOK] = meta
    block_ref[TOK:ROWS, 4 * TOK :] = jnp.zeros((META, grad_ref.shape[1] - 4 * TOK), BF16)


def pack(grad, routes, gates):
    return pl.pallas_call(
        pack_kernel,
        out_shape=jax.ShapeDtypeStruct((ROWS, grad.shape[1]), BF16),
        cost_estimate=pl.CostEstimate(flops=0, bytes_accessed=1 << 20, transcendentals=0),
        name="pack",
    )(grad, routes, gates)


def split(value):
    high = value.astype(BF16)
    return high, (value - high.astype(F32)).astype(BF16)


def turn(order, hidden_ref, turned, sources):
    for j in range(sources // 2):
        pair = [
            hidden_ref[pl.ds(pl.multiple_of(order[2 * j + k] * CAP, CAP), CAP), :] for k in range(2)
        ]
        turned[:, j * 2 * CAP : (j + 1) * 2 * CAP] = jnp.concatenate(pair, axis=0).T


def left(acc, q_ref, total_ref):
    rank = q_ref.shape[1] // 2
    high, low = split(acc)
    both = jnp.dot(high, q_ref[...], preferred_element_type=F32)
    rest = jnp.dot(low, q_ref[:, :rank], preferred_element_type=F32)
    total_ref[...] += both[:, :rank] + (both[:, rank:] + rest)
    return high, low


def product_kernel(count, sources, order, hidden_ref, *refs):
    parts = refs[:count]
    init_ref, q_ref, acc_ref, p_ref, turned = refs[count:]

    @pl.when(pl.program_id(0) == 0)
    def _():
        p_ref[...] = jnp.zeros_like(p_ref)
        turn(order, hidden_ref, turned, sources)

    data = jnp.concatenate([p[...] for p in parts], axis=0)
    acc = init_ref[...].astype(F32) + jnp.dot(turned[...], data, preferred_element_type=F32)
    acc_ref[...] = acc
    left(acc, q_ref, p_ref)


def product(order, hidden, parts, init, q_turned, tile=256):
    rows, width = init.shape
    slots, feats = hidden.shape
    sources = order.shape[0]
    thin = q_turned.shape[1]
    flat = pl.BlockSpec((rows, tile), lambda i, order: (0, i))
    return pl.pallas_call(
        functools.partial(product_kernel, len(parts), sources),
        grid_spec=pltpu.PrefetchScalarGridSpec(
            num_scalar_prefetch=1,
            grid=(width // tile,),
            in_specs=[pl.BlockSpec((slots, feats), lambda i, order: (0, 0))]
            + [pl.BlockSpec((p.shape[0], tile), lambda i, order: (0, i)) for p in parts]
            + [flat, pl.BlockSpec((tile, thin), lambda i, order: (i, 0))],
            out_specs=[flat, pl.BlockSpec((rows, thin // 2), lambda i, order: (0, 0))],
            scratch_shapes=[pltpu.VMEM((feats, sources * CAP), BF16)],
        ),
        out_shape=[
            jax.ShapeDtypeStruct((rows, width), F32),
            jax.ShapeDtypeStruct((rows, thin // 2), F32),
        ],
        cost_estimate=pl.CostEstimate(
            flops=2 * feats * sources * CAP * width,
            bytes_accessed=rows * width * 8 + sources * CAP * (feats + width) * 2,
            transcendentals=0,
        ),
        compiler_params=pltpu.CompilerParams(vmem_limit_bytes=40 << 20),
        name="product",
    )(order, hidden, *parts, init, q_turned)


def left_kernel(count, sources, order, hidden_hbm, *refs):
    parts = refs[:count]
    q_ref, p_ref, out_ref, held, sem = refs[count:]
    copies = [
        pltpu.make_async_copy(
            hidden_hbm.at[pl.ds(pl.multiple_of(order[j] * CAP, CAP), CAP)],
            held.at[pl.ds(j * CAP, CAP)],
            sem.at[j],
        )
        for j in range(sources)
    ]
    for copy in copies:
        copy.start()
    data = jnp.concatenate([p[...] for p in parts], axis=0)
    rank = out_ref.shape[0]
    both = jnp.dot(data, q_ref[...], preferred_element_type=F32)
    high, low = split(both[:, :rank] + both[:, rank:])
    for copy in copies:
        copy.wait()
    more = lax.dot_general(
        jnp.concatenate([high, low], axis=1),
        held[...],
        (((0,), (0,)), ((), ())),
        preferred_element_type=F32,
    )
    out_ref[...] = p_ref[...] + (more[:rank] + more[rank:])


def left_share(order, hidden, parts, q_turned, p_rest):
    vmem = pl.BlockSpec(memory_space=pltpu.VMEM)
    sources = order.shape[0]
    feats = hidden.shape[1]
    return pl.pallas_call(
        functools.partial(left_kernel, len(parts), sources),
        in_specs=[pl.BlockSpec(memory_space=pltpu.SMEM), pl.BlockSpec(memory_space=pl.ANY)]
        + [vmem] * (len(parts) + 2),
        out_specs=vmem,
        out_shape=jax.ShapeDtypeStruct(p_rest.shape, F32),
        scratch_shapes=[
            pltpu.VMEM((sources * CAP, feats), BF16),
            pltpu.SemaphoreType.DMA((sources,)),
        ],
        compiler_params=pltpu.CompilerParams(vmem_limit_bytes=16 << 20),
        name="left_share",
    )(order, hidden, *parts, q_turned, p_rest)


def tail_kernel(count, sources, tile, order, hidden_hbm, *refs):
    parts = refs[:count]
    acc_ref, high_ref, low_ref, held, turned, sem = refs[count:]
    copies = [
        pltpu.make_async_copy(
            hidden_hbm.at[pl.ds(pl.multiple_of(order[j] * CAP, CAP), CAP)],
            held.at[pl.ds(j * CAP, CAP)],
            sem.at[j],
        )
        for j in range(sources)
    ]
    for copy in copies:
        copy.start()
    for copy in copies:
        copy.wait()
    for j in range(0, sources * CAP, 2 * CAP):
        turned[:, j : j + 2 * CAP] = held[j : j + 2 * CAP, :].T

    @pl.loop(0, acc_ref.shape[1] // tile)
    def _(i):
        cols = pl.ds(pl.multiple_of(i * tile, tile), tile)
        data = jnp.concatenate([p[:, cols] for p in parts], axis=0)
        acc = acc_ref[:, cols] + jnp.dot(turned[...], data, preferred_element_type=F32)
        high_ref[:, cols], low_ref[:, cols] = split(acc)


def tail(order, hidden, parts, acc, tile=256):
    rows, width = acc.shape
    feats = hidden.shape[1]
    sources = order.shape[0]
    vmem = pl.BlockSpec(memory_space=pltpu.VMEM)
    return pl.pallas_call(
        functools.partial(tail_kernel, len(parts), sources, tile),
        in_specs=[pl.BlockSpec(memory_space=pltpu.SMEM), pl.BlockSpec(memory_space=pl.ANY)]
        + [vmem] * (len(parts) + 1),
        out_specs=[vmem, vmem],
        scratch_shapes=[
            pltpu.VMEM((sources * CAP, feats), BF16),
            pltpu.VMEM((feats, sources * CAP), BF16),
            pltpu.SemaphoreType.DMA((sources,)),
        ],
        out_shape=[jax.ShapeDtypeStruct((rows, width), BF16)] * 2,
        cost_estimate=pl.CostEstimate(
            flops=2 * feats * sources * CAP * width,
            bytes_accessed=rows * width * 8 + sources * CAP * (feats + width) * 2,
            transcendentals=0,
        ),
        compiler_params=pltpu.CompilerParams(vmem_limit_bytes=32 << 20),
        name="tail",
    )(order, hidden, *parts, acc)


def factors_kernel(a_ref, b_ref, c_ref, d_ref, high_ref, low_ref, p_ref, q_ref, turned_ref):
    current = (a_ref[...] + b_ref[...]) + (c_ref[...] + d_ref[...])
    count = current.shape[0]
    row = lax.broadcasted_iota(jnp.int32, (count, 1), 0)
    for i in range(count):
        vector = current[i : i + 1, :]
        dots = jnp.sum(current * vector, axis=1, keepdims=True)
        norm2 = dots[i : i + 1, :]
        coeffs = jnp.where(row > i, dots / norm2, 0.0)
        scale = jnp.where(row == i, lax.rsqrt(norm2), 1.0)
        current = current * scale - coeffs * vector
    p_ref[...] = current
    p_high, p_low = split(current)
    p_both = jnp.concatenate([p_high, p_low], axis=0)
    turned_ref[...] = jnp.concatenate([p_high, p_both], axis=0).T
    for c in range(0, q_ref.shape[1], 512):
        both = jnp.dot(p_both, high_ref[:, c : c + 512], preferred_element_type=F32)
        rest = jnp.dot(p_high, low_ref[:, c : c + 512], preferred_element_type=F32)
        q_ref[:, c : c + 512] = both[:count] + (both[count:] + rest)


def factors(parts, high, low):
    rank = parts[0].shape[0]
    rows, width = high.shape
    vmem = pl.BlockSpec(memory_space=pltpu.VMEM)
    return pl.pallas_call(
        factors_kernel,
        in_specs=[vmem] * 6,
        out_specs=[vmem] * 3,
        out_shape=[
            jax.ShapeDtypeStruct((rank, rows), F32),
            jax.ShapeDtypeStruct((rank, width), F32),
            jax.ShapeDtypeStruct((rows, 3 * rank), BF16),
        ],
        compiler_params=pltpu.CompilerParams(vmem_limit_bytes=24 << 20),
        name="factors",
    )(*parts, high, low)


def finish_kernel(tile, p_ref, a_ref, b_ref, c_ref, d_ref, high_ref, low_ref, out_hbm, q_ref, held, sems):
    q = (a_ref[...].astype(F32) + b_ref[...].astype(F32)) + (
        c_ref[...].astype(F32) + d_ref[...].astype(F32)
    )
    q = q * 0.125
    q_ref[...] = q
    q_high, q_low = split(q)
    stack = jnp.concatenate([q_high, q_low, q_high], axis=0)
    copies = []
    for c in range(0, high_ref.shape[1], tile):
        approx = jnp.dot(p_ref[...], stack[:, c : c + tile], preferred_element_type=F32)
        acc = high_ref[:, c : c + tile].astype(F32) + low_ref[:, c : c + tile].astype(F32)
        held[:, c : c + tile] = (acc - approx).astype(BF16)
        copy = pltpu.make_async_copy(
            held.at[:, pl.ds(c, tile)], out_hbm.at[:, pl.ds(c, tile)], sems.at[c // tile]
        )
        copy.start()
        copies.append(copy)
    for copy in copies:
        copy.wait()


def finish(p_turned, parts, high, low, tile=256):
    rows, width = high.shape
    rank = parts[0].shape[0]
    vmem = pl.BlockSpec(memory_space=pltpu.VMEM)
    return pl.pallas_call(
        functools.partial(finish_kernel, tile),
        in_specs=[vmem] * 7,
        out_specs=[pl.BlockSpec(memory_space=pl.ANY), vmem],
        out_shape=[
            jax.ShapeDtypeStruct((rows, width), BF16),
            jax.ShapeDtypeStruct((rank, width), F32),
        ],
        scratch_shapes=[
            pltpu.VMEM((rows, width), BF16),
            pltpu.SemaphoreType.DMA((width // tile,)),
        ],
        compiler_params=pltpu.CompilerParams(vmem_limit_bytes=24 << 20),
        name="finish",
    )(p_turned, *parts, high, low)


def partner(value, k):
    return lax.ppermute(value, "rep", [(i, i ^ k) for i in range(8)])


def body(grad_out, gates, routes, hidden, error, q_init):
    me = lax.axis_index("exp").astype(jnp.int32)
    x, z = me // NZ, me % NZ
    ids = jnp.arange(NX, dtype=jnp.int32) * NZ + z
    own = pack(grad_out[0], routes[0].T, gates[0].T)

    b = {0: own}
    parts, order = [], []
    columns = [[i * NZ + k for i in range(NX)] for k in range(NZ)]

    def spread(group, sent):
        parts.append(
            lax.all_to_all(
                sent, "exp", split_axis=0, concat_axis=0, tiled=True, axis_index_groups=columns
            )
        )
        dx = jnp.array([i for i in range(NX) for k in group], jnp.int32)
        dz = jnp.array([k for i in range(NX) for k in group], jnp.int32)
        order.append(dx * NZ + (z - dz) % NZ)

    b[1] = move(b[0], 0, 1)
    b[7] = move(b[0], 0, -1)
    b[2] = move(b[1], 0, 1)
    b[6] = move(b[7], 0, -1)
    b[3] = move(b[2], 0, 1)
    b[5] = move(b[6], 0, -1)
    b[4] = move(b[3], 0, 1)
    spread(GROUPS[0], select([own], ids))
    for group in GROUPS[1:4]:
        spread(group, select([b[k] for k in group], ids))
    held = hidden[0, 0]
    q_turned = jnp.concatenate(split(q_init[0]), axis=0).T
    acc, p_rest = product(jnp.concatenate(order[:3]), held, parts[:3], error[0, 0], q_turned)
    spread(GROUPS[4], select([b[k] for k in GROUPS[4]], ids, (p_rest,)))
    p_rest = left_share(order[3], held, parts[3:4], q_turned, p_rest.T)
    p_local = left_share(order[4], held, parts[4:], q_turned, p_rest)
    p_chip = p_local + partner(p_local, 1)
    p_parts = [p_chip] + [partner(p_chip, k) for k in (2, 4, 6)]
    high, low = tail(jnp.concatenate(order[3:]), held, parts[3:], acc)
    p_hat, q_local, p_turned = factors(p_parts, high, low)
    q_chip = (q_local + partner(q_local, 1)).astype(BF16)
    new_error, q_mean = finish(p_turned, [q_chip] + [partner(q_chip, k) for k in (2, 4, 6)], high, low)
    return new_error[None, None], p_hat[None], q_mean[None]


def solution(mesh):
    return jax.shard_map(
        body,
        mesh=mesh,
        in_specs=(
            P("rep", "exp", None),
            P("rep", "exp", None),
            P("rep", "exp", None),
            P("rep", "exp", None, None),
            P("rep", "exp", None, None),
            P("exp", None, None),
        ),
        out_specs=(P("rep", "exp", None, None), P("exp", None, None), P("exp", None, None)),
        check_vma=False,
    )
```

```python
import functools

import jax
import jax.numpy as jnp
from jax import lax
from jax.experimental import pallas as pl
from jax.experimental.pallas import tpu as pltpu
from jax.sharding import PartitionSpec as P

F32 = jnp.float32
BF16 = jnp.bfloat16

NX, NZ = 4, 8
TOK = 128
CAP = 64
META = 8
ROWS = TOK + META
GROUPS = ((0,), (1, 7), (2, 6), (3, 5), (4,))


def move(block, dx, dz):
    pairs = []
    for x in range(NX):
        for z in range(NZ):
            pairs.append((x * NZ + z, ((x + dx) % NX) * NZ + (z + dz) % NZ))
    return lax.ppermute(block, "exp", pairs)


def select_kernel(counts, experts, ids_ref, *refs):
    blocks, out_ref = refs[: len(counts)], refs[-1]
    total = sum(counts) * CAP
    row = lax.broadcasted_iota(jnp.int32, (TOK, TOK), 0)
    col = lax.broadcasted_iota(jnp.int32, (TOK, TOK), 1)
    before = jnp.where(row < col, 1.0, 0.0).astype(BF16)
    slot = lax.broadcasted_iota(jnp.int32, (CAP, TOK), 0).astype(F32)
    place = 0
    for ref, count in zip(blocks, counts):
        for b in range(count):
            base = b * ROWS
            meta = ref[base + TOK : base + ROWS, 0 : 4 * TOK].astype(F32)
            routes = meta[:, 0:TOK]
            gates = (meta[:, TOK : 2 * TOK] + meta[:, 2 * TOK : 3 * TOK]) + meta[:, 3 * TOK :]
            gate, live = [], []
            for e in range(experts):
                match = routes == ids_ref[e].astype(F32)
                gate.append(jnp.sum(jnp.where(match, gates, 0.0), axis=0, keepdims=True))
                live.append(jnp.sum(jnp.where(match, 1.0, 0.0), axis=0, keepdims=True))
            alive = jnp.concatenate(live + [jnp.zeros((8 - experts, TOK), F32)], axis=0)
            position = jnp.dot(alive.astype(BF16), before, preferred_element_type=F32)
            picks, scales = [], []
            for e in range(experts):
                pick = jnp.where((slot == position[e : e + 1]) & (live[e] > 0.0), 1.0, 0.0)
                picks.append(pick)
                scales.append(jnp.sum(pick * gate[e], axis=1, keepdims=True))
            pick = jnp.concatenate(picks, axis=0).astype(BF16)
            scale = jnp.concatenate(scales, axis=0)
            for c in range(0, ref.shape[1], 512):
                rows = jnp.dot(
                    pick, ref[base : base + TOK, c : c + 512], preferred_element_type=F32
                )
                rows = (rows * scale).astype(BF16)
                for e in range(experts):
                    first = e * total + place
                    out_ref[first : first + CAP, c : c + 512] = rows[e * CAP : (e + 1) * CAP]
            place += CAP


def select(blocks, ids, after=()):
    counts = tuple(b.shape[0] // ROWS for b in blocks)
    width = blocks[0].shape[1]
    experts = ids.shape[0]
    total = sum(counts)
    return pl.pallas_call(
        functools.partial(select_kernel, counts, experts),
        in_specs=[pl.BlockSpec(memory_space=pltpu.SMEM)]
        + [pl.BlockSpec(memory_space=pltpu.VMEM)] * len(blocks)
        + [pl.BlockSpec(memory_space=pl.ANY)] * len(after),
        out_specs=pl.BlockSpec(memory_space=pltpu.VMEM),
        out_shape=jax.ShapeDtypeStruct((experts * total * CAP, width), BF16),
        cost_estimate=pl.CostEstimate(
            flops=2 * total * experts * CAP * TOK * width,
            bytes_accessed=total * (ROWS + CAP * experts) * width * 2,
            transcendentals=0,
        ),
        compiler_params=pltpu.CompilerParams(vmem_limit_bytes=32 << 20),
        name="select",
    )(ids, *blocks, *after)


def pack_kernel(grad_ref, routes_ref, gates_ref, block_ref):
    gates = gates_ref[...]
    high = gates.astype(BF16)
    rest = gates - high.astype(F32)
    mid = rest.astype(BF16)
    low = (rest - mid.astype(F32)).astype(BF16)
    meta = jnp.concatenate([routes_ref[...].astype(F32).astype(BF16), high, mid, low], axis=1)
    block_ref[0:TOK, :] = grad_ref[...]
    block_ref[TOK:ROWS, 0 : 4 * TOK] = meta
    block_ref[TOK:ROWS, 4 * TOK :] = jnp.zeros((META, grad_ref.shape[1] - 4 * TOK), BF16)


def pack(grad, routes, gates):
    return pl.pallas_call(
        pack_kernel,
        out_shape=jax.ShapeDtypeStruct((ROWS, grad.shape[1]), BF16),
        cost_estimate=pl.CostEstimate(flops=0, bytes_accessed=1 << 20, transcendentals=0),
        name="pack",
    )(grad, routes, gates)


def split(value):
    high = value.astype(BF16)
    return high, (value - high.astype(F32)).astype(BF16)


def turn(order, hidden_ref, turned, sources):
    for j in range(sources // 2):
        pair = [
            hidden_ref[pl.ds(pl.multiple_of(order[2 * j + k] * CAP, CAP), CAP), :] for k in range(2)
        ]
        turned[:, j * 2 * CAP : (j + 1) * 2 * CAP] = jnp.concatenate(pair, axis=0).T


def left(acc, q_ref, total_ref):
    rank = q_ref.shape[1] // 2
    high, low = split(acc)
    both = jnp.dot(high, q_ref[...], preferred_element_type=F32)
    rest = jnp.dot(low, q_ref[:, :rank], preferred_element_type=F32)
    total_ref[...] += both[:, :rank] + (both[:, rank:] + rest)
    return high, low


def product_kernel(count, sources, order, hidden_ref, *refs):
    parts = refs[:count]
    init_ref, q_ref, acc_ref, p_ref, turned = refs[count:]

    @pl.when(pl.program_id(0) == 0)
    def _():
        p_ref[...] = jnp.zeros_like(p_ref)
        turn(order, hidden_ref, turned, sources)

    data = jnp.concatenate([p[...] for p in parts], axis=0)
    acc = init_ref[...].astype(F32) + jnp.dot(turned[...], data, preferred_element_type=F32)
    acc_ref[...] = acc
    left(acc, q_ref, p_ref)


def product(order, hidden, parts, init, q_turned, tile=256):
    rows, width = init.shape
    slots, feats = hidden.shape
    sources = order.shape[0]
    thin = q_turned.shape[1]
    flat = pl.BlockSpec((rows, tile), lambda i, order: (0, i))
    return pl.pallas_call(
        functools.partial(product_kernel, len(parts), sources),
        grid_spec=pltpu.PrefetchScalarGridSpec(
            num_scalar_prefetch=1,
            grid=(width // tile,),
            in_specs=[pl.BlockSpec((slots, feats), lambda i, order: (0, 0))]
            + [pl.BlockSpec((p.shape[0], tile), lambda i, order: (0, i)) for p in parts]
            + [flat, pl.BlockSpec((tile, thin), lambda i, order: (i, 0))],
            out_specs=[flat, pl.BlockSpec((rows, thin // 2), lambda i, order: (0, 0))],
            scratch_shapes=[pltpu.VMEM((feats, sources * CAP), BF16)],
        ),
        out_shape=[
            jax.ShapeDtypeStruct((rows, width), F32),
            jax.ShapeDtypeStruct((rows, thin // 2), F32),
        ],
        cost_estimate=pl.CostEstimate(
            flops=2 * feats * sources * CAP * width,
            bytes_accessed=rows * width * 8 + sources * CAP * (feats + width) * 2,
            transcendentals=0,
        ),
        compiler_params=pltpu.CompilerParams(vmem_limit_bytes=40 << 20),
        name="product",
    )(order, hidden, *parts, init, q_turned)


def left_kernel(count, sources, order, hidden_hbm, *refs):
    parts = refs[:count]
    q_ref, p_ref, out_ref, held, sem = refs[count:]
    copies = [
        pltpu.make_async_copy(
            hidden_hbm.at[pl.ds(pl.multiple_of(order[j] * CAP, CAP), CAP)],
            held.at[pl.ds(j * CAP, CAP)],
            sem.at[j],
        )
        for j in range(sources)
    ]
    for copy in copies:
        copy.start()
    data = jnp.concatenate([p[...] for p in parts], axis=0)
    rank = out_ref.shape[0]
    both = jnp.dot(data, q_ref[...], preferred_element_type=F32)
    high, low = split(both[:, :rank] + both[:, rank:])
    for copy in copies:
        copy.wait()
    more = lax.dot_general(
        jnp.concatenate([high, low], axis=1),
        held[...],
        (((0,), (0,)), ((), ())),
        preferred_element_type=F32,
    )
    out_ref[...] = p_ref[...] + (more[:rank] + more[rank:])


def left_share(order, hidden, parts, q_turned, p_rest):
    vmem = pl.BlockSpec(memory_space=pltpu.VMEM)
    sources = order.shape[0]
    feats = hidden.shape[1]
    return pl.pallas_call(
        functools.partial(left_kernel, len(parts), sources),
        in_specs=[pl.BlockSpec(memory_space=pltpu.SMEM), pl.BlockSpec(memory_space=pl.ANY)]
        + [vmem] * (len(parts) + 2),
        out_specs=vmem,
        out_shape=jax.ShapeDtypeStruct(p_rest.shape, F32),
        scratch_shapes=[
            pltpu.VMEM((sources * CAP, feats), BF16),
            pltpu.SemaphoreType.DMA((sources,)),
        ],
        compiler_params=pltpu.CompilerParams(vmem_limit_bytes=16 << 20),
        name="left_share",
    )(order, hidden, *parts, q_turned, p_rest)


def turn_kernel(sources, order, hidden_ref, after_ref, out_ref):
    turn(order, hidden_ref, out_ref, sources)


def turn_last(order, hidden, after):
    vmem, far = pl.BlockSpec(memory_space=pltpu.VMEM), pl.BlockSpec(memory_space=pl.ANY)
    feats = hidden.shape[1]
    sources = order.shape[0]
    return pl.pallas_call(
        functools.partial(turn_kernel, sources),
        in_specs=[pl.BlockSpec(memory_space=pltpu.SMEM), vmem, far],
        out_specs=vmem,
        out_shape=jax.ShapeDtypeStruct((feats, sources * CAP), BF16),
        cost_estimate=pl.CostEstimate(flops=0, bytes_accessed=4 << 20, transcendentals=0),
        compiler_params=pltpu.CompilerParams(vmem_limit_bytes=16 << 20),
        name="turn_last",
    )(order, hidden, after)


def tail_kernel(count, tile, turned, *refs):
    parts = refs[:count]
    acc_ref, high_ref, low_ref = refs[count:]

    @pl.loop(0, acc_ref.shape[1] // tile)
    def _(i):
        cols = pl.ds(pl.multiple_of(i * tile, tile), tile)
        data = jnp.concatenate([p[:, cols] for p in parts], axis=0)
        acc = acc_ref[:, cols] + jnp.dot(turned[...], data, preferred_element_type=F32)
        high_ref[:, cols], low_ref[:, cols] = split(acc)


def tail(turned, parts, acc, tile=256):
    rows, width = acc.shape
    depth = turned.shape[1]
    vmem = pl.BlockSpec(memory_space=pltpu.VMEM)
    return pl.pallas_call(
        functools.partial(tail_kernel, len(parts), tile),
        in_specs=[vmem] * (len(parts) + 2),
        out_specs=[vmem, vmem],
        out_shape=[jax.ShapeDtypeStruct((rows, width), BF16)] * 2,
        cost_estimate=pl.CostEstimate(
            flops=2 * rows * depth * width,
            bytes_accessed=rows * width * 8 + depth * (rows + width) * 2,
            transcendentals=0,
        ),
        compiler_params=pltpu.CompilerParams(vmem_limit_bytes=24 << 20),
        name="tail",
    )(turned, *parts, acc)


def factors_kernel(a_ref, b_ref, c_ref, d_ref, high_ref, low_ref, p_ref, q_ref, turned_ref):
    current = (a_ref[...] + b_ref[...]) + (c_ref[...] + d_ref[...])
    count = current.shape[0]
    row = lax.broadcasted_iota(jnp.int32, (count, 1), 0)
    for i in range(count):
        vector = current[i : i + 1, :]
        dots = jnp.sum(current * vector, axis=1, keepdims=True)
        norm2 = dots[i : i + 1, :]
        coeffs = jnp.where(row > i, dots / norm2, 0.0)
        scale = jnp.where(row == i, lax.rsqrt(norm2), 1.0)
        current = current * scale - coeffs * vector
    p_ref[...] = current
    p_high, p_low = split(current)
    p_both = jnp.concatenate([p_high, p_low], axis=0)
    turned_ref[...] = jnp.concatenate([p_high, p_both], axis=0).T
    for c in range(0, q_ref.shape[1], 512):
        both = jnp.dot(p_both, high_ref[:, c : c + 512], preferred_element_type=F32)
        rest = jnp.dot(p_high, low_ref[:, c : c + 512], preferred_element_type=F32)
        q_ref[:, c : c + 512] = both[:count] + (both[count:] + rest)


def factors(parts, high, low):
    rank = parts[0].shape[0]
    rows, width = high.shape
    vmem = pl.BlockSpec(memory_space=pltpu.VMEM)
    return pl.pallas_call(
        factors_kernel,
        in_specs=[vmem] * 6,
        out_specs=[vmem] * 3,
        out_shape=[
            jax.ShapeDtypeStruct((rank, rows), F32),
            jax.ShapeDtypeStruct((rank, width), F32),
            jax.ShapeDtypeStruct((rows, 3 * rank), BF16),
        ],
        compiler_params=pltpu.CompilerParams(vmem_limit_bytes=24 << 20),
        name="factors",
    )(*parts, high, low)


def finish_kernel(tile, p_ref, a_ref, b_ref, c_ref, d_ref, high_ref, low_ref, out_hbm, q_ref, held, sems):
    q = (a_ref[...].astype(F32) + b_ref[...].astype(F32)) + (
        c_ref[...].astype(F32) + d_ref[...].astype(F32)
    )
    q = q * 0.125
    q_ref[...] = q
    q_high, q_low = split(q)
    stack = jnp.concatenate([q_high, q_low, q_high], axis=0)
    copies = []
    for c in range(0, high_ref.shape[1], tile):
        approx = jnp.dot(p_ref[...], stack[:, c : c + tile], preferred_element_type=F32)
        acc = high_ref[:, c : c + tile].astype(F32) + low_ref[:, c : c + tile].astype(F32)
        held[:, c : c + tile] = (acc - approx).astype(BF16)
        copy = pltpu.make_async_copy(
            held.at[:, pl.ds(c, tile)], out_hbm.at[:, pl.ds(c, tile)], sems.at[c // tile]
        )
        copy.start()
        copies.append(copy)
    for copy in copies:
        copy.wait()


def finish(p_turned, parts, high, low, tile=256):
    rows, width = high.shape
    rank = parts[0].shape[0]
    vmem = pl.BlockSpec(memory_space=pltpu.VMEM)
    return pl.pallas_call(
        functools.partial(finish_kernel, tile),
        in_specs=[vmem] * 7,
        out_specs=[pl.BlockSpec(memory_space=pl.ANY), vmem],
        out_shape=[
            jax.ShapeDtypeStruct((rows, width), BF16),
            jax.ShapeDtypeStruct((rank, width), F32),
        ],
        scratch_shapes=[
            pltpu.VMEM((rows, width), BF16),
            pltpu.SemaphoreType.DMA((width // tile,)),
        ],
        compiler_params=pltpu.CompilerParams(vmem_limit_bytes=24 << 20),
        name="finish",
    )(p_turned, *parts, high, low)


def partner(value, k):
    return lax.ppermute(value, "rep", [(i, i ^ k) for i in range(8)])


def body(grad_out, gates, routes, hidden, error, q_init):
    me = lax.axis_index("exp").astype(jnp.int32)
    x, z = me // NZ, me % NZ
    ids = jnp.arange(NX, dtype=jnp.int32) * NZ + z
    own = pack(grad_out[0], routes[0].T, gates[0].T)

    b = {0: own}
    parts, order = [], []
    columns = [[i * NZ + k for i in range(NX)] for k in range(NZ)]

    def spread(group, sent):
        parts.append(
            lax.all_to_all(
                sent, "exp", split_axis=0, concat_axis=0, tiled=True, axis_index_groups=columns
            )
        )
        dx = jnp.array([i for i in range(NX) for k in group], jnp.int32)
        dz = jnp.array([k for i in range(NX) for k in group], jnp.int32)
        order.append(dx * NZ + (z - dz) % NZ)

    b[1] = move(b[0], 0, 1)
    b[7] = move(b[0], 0, -1)
    b[2] = move(b[1], 0, 1)
    b[6] = move(b[7], 0, -1)
    b[3] = move(b[2], 0, 1)
    b[5] = move(b[6], 0, -1)
    b[4] = move(b[3], 0, 1)
    spread(GROUPS[0], select([own], ids))
    held = hidden[0, 0]
    dx = jnp.array([i for group in GROUPS[3:] for i in range(NX) for k in group], jnp.int32)
    dz = jnp.array([k for group in GROUPS[3:] for i in range(NX) for k in group], jnp.int32)
    turned = turn_last(dx * NZ + (z - dz) % NZ, held, own)
    for group, after in zip(GROUPS[1:4], ((), (), (turned,))):
        spread(group, select([b[k] for k in group], ids, after))
    q_turned = jnp.concatenate(split(q_init[0]), axis=0).T
    acc, p_rest = product(jnp.concatenate(order[:3]), held, parts[:3], error[0, 0], q_turned)
    spread(GROUPS[4], select([b[k] for k in GROUPS[4]], ids, (p_rest,)))
    p_rest = left_share(order[3], held, parts[3:4], q_turned, p_rest.T)
    p_local = left_share(order[4], held, parts[4:], q_turned, p_rest)
    p_chip = p_local + partner(p_local, 1)
    p_parts = [p_chip] + [partner(p_chip, k) for k in (2, 4, 6)]
    high, low = tail(turned, parts[3:], acc)
    p_hat, q_local, p_turned = factors(p_parts, high, low)
    q_chip = (q_local + partner(q_local, 1)).astype(BF16)
    new_error, q_mean = finish(p_turned, [q_chip] + [partner(q_chip, k) for k in (2, 4, 6)], high, low)
    return new_error[None, None], p_hat[None], q_mean[None]


def solution(mesh):
    return jax.shard_map(
        body,
        mesh=mesh,
        in_specs=(
            P("rep", "exp", None),
            P("rep", "exp", None),
            P("rep", "exp", None),
            P("rep", "exp", None, None),
            P("rep", "exp", None, None),
            P("exp", None, None),
        ),
        out_specs=(P("rep", "exp", None, None), P("exp", None, None), P("exp", None, None)),
        check_vma=False,
    )
```
